256 devices in a mesh: ops: 8 (over z), sec: 32 (over y, x, core).
Axes of the slice: x: 4, y: 4, z: 8, core: 2. Of those that a mesh axis runs over, the one named last changes fastest.
Arguments:
- wavefunction: bfloat16 [2, 1024, 128, 128], P(None, 'sec'), may hold values from -6 to 6
- right_number: int32 [1024, 1], P('sec'), may hold values from 0 to 31; in each aligned block of 32 rows (0 to 31, 32 to 63, ...) at most 2 rows name the same one
- left_dim: int32 [32], P('sec'), may hold values from 64 to 128, as said below
- right_dim: int32 [32], P('sec'), may hold values from 64 to 128, as said below
- left_ops: bfloat16 [32, 32, 128, 128], P('ops', 'sec'), may hold values from -0.09375 to 0.09375
- right_ops: bfloat16 [32, 32, 128, 128], P('ops', 'sec'), may hold values from -0.5 to 0.5
- set_kind: int32 [32], P('ops'), may hold values from 0 to 1
Outputs:
- sigma: bfloat16 [2, 1024, 128, 128], P(None, 'sec')
- subspace: float32 [2, 2], replicated
The draws below stay inside these ranges and needn't reach their ends.
Inputs may be any that keep to these rules, and one draw needn't show every extreme that they name: `right_number`: no more than 2 of the sectors s with the same s // 32 share a right quantum number; some such set has exactly 2. `left_dim`: some left quantum number has the full 128. `right_dim`: some right quantum number has the full 128.
All inputs are finite; a program needn't handle non-finite values.
Results may differ from the reference program's by a relative error of at most 0.005.
Values may be sent and summed in bfloat16 or wider, within the bound.
A program may use at most 128 MiB of HBM per device.

```python
import math
import jax
import jax.numpy as jnp
import numpy as np
from jax import lax

BLK = 128
SEC_DEV = 32
K_DEV = 4
NVEC = 2
CAP = 2
SECTORS = 1024
LEFTQ = 32
RIGHT_QUANTA = 32
TERMS = 32
N_OPS = 8


def block_sizes(key, count):
    values = jax.random.randint(key, (count,), BLK // 2, BLK + 1, dtype=jnp.int32)
    chosen = jax.random.randint(jax.random.fold_in(key, 7), (), 0, count, dtype=jnp.int32)
    return jnp.where(jnp.arange(count, dtype=jnp.int32) == chosen, jnp.int32(BLK), values)


def draw_left_dim(key, part):
    key = jax.random.fold_in(key, 11)
    return block_sizes(key, LEFTQ)


def draw_right_dim(key, part):
    key = jax.random.fold_in(key, 12)
    return block_sizes(key, RIGHT_QUANTA)


def plant(drawn, key, least, high):
    place = [jax.random.randint(jax.random.fold_in(key, axis), (), 0, length) for axis, length in enumerate(drawn.shape)]
    widest = drawn.shape.index(max(drawn.shape))
    next_to = place[:widest] + [(place[widest] + 1) % drawn.shape[widest]] + place[widest + 1:]
    return drawn.at[tuple(place)].set(least).at[tuple(next_to)].set(high)


def shard_levels(rng, shape, shards, least, largest):
    def one(position, blocks):
        steps = jax.random.uniform(jax.random.fold_in(jax.random.fold_in(rng, 6), position), (blocks,), jnp.float32, least / len(shards), largest / len(shards))
        return jnp.repeat(jnp.exp(steps), shape[position] // blocks).reshape((-1,) + (1,) * (len(shape) - position - 1))

    gain = one(*shards[0])
    for cut in shards[1:]:
        gain = gain * one(*cut)
    return gain


def shared_out(key, own, number, rows, amount, top, limit, lean):
    order = jax.random.permutation(key, amount)
    crowded, ordinary = shares(amount, rows * top, limit, lean, True), shares(amount, rows * top, limit, lean, False)
    places = jnp.arange(amount)

    def named(sizes, turn):
        used = int((sizes > 0).sum())
        fixed = max(1, used // 4)
        shifted = fixed + (places - fixed + turn * (used - fixed)) % max(1, amount - fixed)
        return jnp.zeros((amount,), jnp.int32).at[order[jnp.where(places < fixed, places, shifted)]].set(jnp.asarray(sizes, jnp.int32))

    sizes = jnp.where(number % 4 == 0, named(crowded, number // 4), named(ordinary, number - number // 4 - 1))
    mixed = jax.random.permutation(jax.random.fold_in(own, 3), amount)
    source_of, receiver = mixed[0:amount // 2 * 2:2], mixed[1:amount // 2 * 2:2]
    room = jnp.minimum(sizes[source_of] - 1, limit - sizes[receiver]) // 2
    room = jnp.where((source_of == order[0]) | (receiver == order[0]) | (sizes[receiver] == 0), 0, jnp.maximum(room, 0))
    shifted = jax.random.randint(jax.random.fold_in(own, 4), (amount // 2,), 0, 1 << 20) % (room + 1)
    sizes = sizes.at[source_of].add(-shifted).at[receiver].add(shifted)
    labels = jnp.searchsorted(jnp.cumsum(sizes), jnp.arange(rows * top), side="right").astype(jnp.int32)
    listing = labels.reshape(top, rows).T
    listing = listing[jax.random.permutation(jax.random.fold_in(own, 1), rows)]
    turn = jax.random.randint(jax.random.fold_in(own, 2), (rows, 1), 0, top)
    return jnp.take_along_axis(listing, (jnp.arange(top)[None, :] + turn) % top, axis=1)


def shares(count, total, most, lean, full):
    weights = [(1 << 20) // math.isqrt(standing ** lean) + 1 for standing in range(1, count + 1)]
    largest = most if full else min(most, max(-(-total // count), total * weights[0] // sum(weights)))
    least = 1 if total - largest >= count - 1 else 0
    counts, spare = [largest] + [least] * (count - 1), total - largest - least * (count - 1)
    while spare > 0:
        movable = [i for i in range(1, count) if counts[i] < largest] or [i for i in range(1, count) if counts[i] < most]
        whole, left = sum([weights[i] for i in movable]), spare
        for i in movable:
            more = min(most - counts[i], max(1, left * weights[i] // whole), spare)
            counts[i] = counts[i] + more
            spare = spare - more
    return np.array(counts)


def normal_values(stream_key, extent, scale, most, shards=(), held_as=jnp.bfloat16):
    result = jax.random.normal(stream_key, extent, jnp.float32) * scale
    if len(shards) > 0:
        result = shard_levels(stream_key, extent, shards, -0.22, 0.18) * result
    return jnp.clip(result, min=-most, max=most).astype(held_as)


def setup_inputs(seed: int = 0) -> dict:
    arg_keys = jax.random.split(jax.random.key(seed), 8)
    wavefunction = normal_values(arg_keys[0], (NVEC, SECTORS, BLK, BLK), 1.0, 6.0, ((1, 32),))
    right_number_keys = jax.random.split(jax.random.fold_in(arg_keys[1], 1), SECTORS // SEC_DEV)
    right_number_turns = jax.random.permutation(jax.random.fold_in(arg_keys[1], 3), SECTORS // SEC_DEV)
    right_number = jax.vmap(lambda own, number: shared_out(jax.random.fold_in(arg_keys[1], 2), own, number, SEC_DEV, RIGHT_QUANTA, 1, CAP, 2))(right_number_keys, right_number_turns).reshape((SECTORS, 1))
    left_dim = draw_left_dim(jax.random.fold_in(arg_keys[7], 71), 0)
    right_dim = draw_right_dim(jax.random.fold_in(arg_keys[7], 71), 0)
    left_ops = normal_values(arg_keys[4], (TERMS, LEFTQ, BLK, BLK), (BLK * TERMS) ** -0.5, 0.09375, ((0, 8), (1, 32)))
    right_ops = normal_values(arg_keys[5], (TERMS, RIGHT_QUANTA, BLK, BLK), BLK ** -0.5, 0.5, ((0, 8), (1, 32)))
    set_kind = plant(jax.random.randint(arg_keys[6], (TERMS,), 0, 2), jax.random.fold_in(arg_keys[6], 1), 0, 1).astype(jnp.int32)
    return {"wavefunction": wavefunction, "right_number": right_number, "left_dim": left_dim, "right_dim": right_dim, "left_ops": left_ops, "right_ops": right_ops, "set_kind": set_kind}


def reference(wavefunction, right_number, left_dim, right_dim, left_ops, right_ops, set_kind):
    lanes = jnp.arange(BLK, dtype=jnp.int32)
    flipped = jnp.where(set_kind[:, None, None, None] == 1, jnp.swapaxes(left_ops, 2, 3), left_ops)

    def one_sector(index):
        left_num = index // SEC_DEV
        right_num = right_number[index, 0]
        row_keep = lanes < left_dim[left_num]
        column_retained = lanes < right_dim[right_num]
        block = wavefunction[:, index]
        masked_block = jnp.where(row_keep[None, :, None] & column_retained[None, None, :], block, jnp.zeros_like(block))
        right_present = right_ops[:, right_num].astype(jnp.float32)
        left_present = flipped[:, left_num].astype(jnp.float32).reshape(N_OPS, K_DEV, BLK, BLK)
        inner_product = jnp.einsum('ojz,wzf->owjf', masked_block.astype(jnp.float32), right_present).astype(jnp.bfloat16)
        inner_product = inner_product.astype(jnp.float32).reshape(wavefunction.shape[0], N_OPS, K_DEV, BLK, BLK)
        partial_value = jnp.einsum('gkea,vgkac->vgec', left_present, inner_product)
        partial_value = jnp.where(column_retained[None, None, None, :], partial_value, 0.0)
        total = lax.optimization_barrier(jnp.sum(partial_value, axis=1))
        total = jnp.where(row_keep[None, :, None], total, 0.0)
        return total.astype(jnp.bfloat16)
    stacked = lax.map(one_sector, jnp.arange(SECTORS, dtype=jnp.int32))
    sigma = jnp.swapaxes(stacked, 0, 1)
    scale = 1.0 / jnp.sqrt(jnp.float32(SECTORS * BLK * BLK))
    subspace = jnp.einsum('vsab,wsab->vw', wavefunction.astype(jnp.float32), sigma.astype(jnp.float32)) * scale
    return (sigma, subspace)
```

```python
import functools
import math

import jax
import jax.numpy as jnp
from jax import lax
from jax.experimental import pallas as pl
from jax.experimental.pallas import tpu as pltpu
from jax.sharding import PartitionSpec as P

MESH = pl.DeviceIdType.MESH
BF16 = jnp.bfloat16
F32 = jnp.float32


def remote(src, dst, send, recv, device):
    return pltpu.make_async_remote_copy(
        src_ref=src, dst_ref=dst, send_sem=send, recv_sem=recv, device_id=device, device_id_type=MESH
    )


class Ring:
    def __init__(self, n, me, device, slot, half, send, recv):
        self.n, self.me, self.device = n, me, device
        self.slot, self.half, self.send, self.recv = slot, half, send, recv
        self.sent = []

    def at(self, offset):
        return lax.rem(self.me + (offset + self.n), self.n)

    def ref(self, offset, distance, way):
        if 2 * distance == self.n:
            return self.half(self.at(offset), way)
        return self.slot(self.at(offset))

    def pass_on(self, distance, way):
        step = 1 if way == 0 else -1
        block = self.ref(-step * (distance - 1), distance, way)
        index = way * (self.n // 2) + distance - 1
        copy = remote(block, block, self.send(index), self.recv(index), self.device(self.at(step)))
        copy.start()
        self.sent.append(copy)

    def start(self):
        if self.n > 1:
            self.pass_on(1, 0)
            self.pass_on(1, 1)

    def step(self, distance):
        if 2 * distance > self.n:
            return
        for way in range(2):
            step = 1 if way == 0 else -1
            block = self.ref(-step * distance, distance, way)
            index = way * (self.n // 2) + distance - 1
            remote(block, block, self.send(index), self.recv(index), self.device(self.at(step))).wait_recv()
            if 2 * (distance + 1) <= self.n:
                self.pass_on(distance + 1, way)

    def finish(self):
        for copy in self.sent:
            copy.wait_send()
        self.sent = []


def kernel(
    planes, side, chunk,
    w_hbm, number, left_dim, right_dim, left_ops, right_ops, kind,
    out, sub,
    w, rt, rg, lg, inner, sg, turned, red,
    w_sem, a2a_send, a2a_recv, ring_send, ring_recv, sib_send, sib_recv, red_send, red_recv,
):
    terms, width = left_ops.shape[0], left_ops.shape[-1]
    nvec, sectors = w.shape[0], w.shape[1]
    part = width // planes
    chunks = sectors // chunk
    rows = nvec * part
    plane = lax.axis_index("ops")
    place = lax.axis_index("sec")
    core = lax.rem(place, 2)
    chip = place // 2
    px, py = lax.rem(chip, side), chip // side
    first = px * (1 - core) + py * core
    second = py * (1 - core) + px * core

    def sector_of(one, two, c):
        x = one * (1 - c) + two * c
        y = two * (1 - c) + one * c
        return 2 * (y * side + x) + c

    def shift(base, offset, n):
        return lax.rem(base + (offset + n), n)

    above = [{"ops": shift(plane, d, planes)} for d in range(1, planes)]
    along = [{"sec": sector_of(shift(first, d, side), second, core)} for d in range(1, side)]
    across = [{"sec": sector_of(first, shift(second, d, side), core)} for d in range(1, side)]
    sibling = {"sec": place + 1 - 2 * core}

    barrier = pltpu.get_barrier_semaphore()
    partners = above + along + across + [sibling]
    for device in partners:
        pl.semaphore_signal(barrier, inc=1, device_id=device, device_id_type=MESH)

    w_copy = pltpu.make_async_copy(w_hbm, w, w_sem)
    w_copy.start()

    lane = lax.broadcasted_iota(jnp.int32, (width, width), 1)
    sub_lane = lax.broadcasted_iota(jnp.int32, (width, width), 0)
    right_keep = (lane < right_dim[0]) & (sub_lane < right_dim[0])
    left_keep = (lane < left_dim[0]) & (sub_lane < left_dim[0])
    for k in range(terms):
        block = jnp.where(right_keep, right_ops[k, 0].astype(F32), 0.0).T.astype(BF16)
        for o in range(planes):
            rt[o, k * part:(k + 1) * part] = block[o * part:(o + 1) * part]
    for k in range(terms):
        block = jnp.where(left_keep, left_ops[k, 0].astype(F32), 0.0)
        normal = (jnp.zeros((width, width), jnp.int32) + kind[k]) == 0
        lg[plane, k * width:(k + 1) * width] = jnp.where(normal, block.T, block).astype(BF16)
    rg[place, pl.ds(pl.multiple_of(plane * (terms * part), terms * part), terms * part)] = rt[plane]

    pl.semaphore_wait(barrier, len(partners))

    def a2a(d):
        to = shift(plane, d, planes)
        piece = rg.at[place, pl.ds(pl.multiple_of(plane * (terms * part), terms * part), terms * part)]
        return remote(rt.at[to], piece, a2a_send.at[d - 1], a2a_recv.at[d - 1], {"ops": to})

    def a2a_arrival(d):
        source = shift(plane, -d, planes)
        piece = rg.at[place, pl.ds(pl.multiple_of(source * (terms * part), terms * part), terms * part)]
        return remote(piece, piece, a2a_send.at[d - 1], a2a_recv.at[d - 1], {"ops": shift(plane, d, planes)})

    slices = [a2a(d) for d in range(1, planes)]
    for copy in slices:
        copy.start()

    count = [0]

    def ring(n, me, device, slot, half):
        index = count[0]
        count[0] += 1
        return Ring(n, me, device, slot, half, lambda i: ring_send.at[index, i], lambda i: ring_recv.at[index, i])

    big = rg.shape[1]

    def half_rows(h, total):
        return pl.ds(h * (total // 2), total // 2)

    left = ring(
        planes, plane, lambda q: {"ops": q}, lambda q: lg.at[q], lambda q, h: lg.at[q, half_rows(h, lg.shape[1])]
    )
    one = ring(
        side, first, lambda q: {"sec": sector_of(q, second, core)},
        lambda q: rg.at[sector_of(q, second, core)],
        lambda q, h: rg.at[sector_of(q, second, core), half_rows(h, big)],
    )

    def second_ring(offset):
        line = shift(first, offset, side)
        return ring(
            side, second, lambda q: {"sec": sector_of(first, q, core)},
            lambda q: rg.at[sector_of(line, q, core)],
            lambda q, h: rg.at[sector_of(line, q, core), half_rows(h, big)],
        )

    two = [second_ring(offset) for offset in range(side)]
    handed = []

    def hand(d1, d2):
        block = rg.at[sector_of(shift(first, d1, side), shift(second, d2, side), core)]
        index = d1 * side + d2
        copy = remote(block, block, sib_send.at[index], sib_recv.at[index], sibling)
        copy.start()
        handed.append(copy)

    def handed_over(d1, d2):
        block = rg.at[sector_of(shift(second, d1, side), shift(first, d2, side), 1 - core)]
        index = d1 * side + d2
        remote(block, block, sib_send.at[index], sib_recv.at[index], sibling).wait_recv()

    left.start()
    for d in range(1, planes):
        a2a_arrival(d).wait_recv()
    one.start()
    two[0].start()
    hand(0, 0)
    if side == 4:
        one.step(1)
        two[1].start()
        two[3].start()
        hand(1, 0)
        hand(3, 0)
        two[0].step(1)
        hand(0, 1)
        hand(0, 3)
        left.step(1)
        one.step(2)
        two[2].start()
        hand(2, 0)
        for j in (1, 3):
            two[j].step(1)
            hand(j, 1)
            hand(j, 3)
        left.step(2)
        two[0].step(2)
        hand(0, 2)
        two[2].step(1)
        hand(2, 1)
        hand(2, 3)
        left.step(3)
        for j in (1, 3, 2):
            two[j].step(2)
            hand(j, 2)
    else:
        for d in (1, 2, 3):
            left.step(d)
    left.step(4)
    for d1 in range(side):
        for d2 in range(side):
            handed_over(d1, d2)
    w_copy.wait()

    chunk_rows = chunk * rows

    def sigma_ring(j):
        return ring(
            planes, plane, lambda q: {"ops": q}, lambda q: sg.at[j, q],
            lambda q, h: sg.at[j, q, half_rows(h, chunk_rows)],
        )

    sigma_rings = [sigma_ring(j) for j in range(chunks)]
    all_terms = terms * planes

    def compute(j):
        for i in range(chunk):
            s = j * chunk + i
            right = rg[number[s, 0]]
            block = w[:, s].reshape(nvec * width, width)
            product = lax.dot_general(
                right, block, (((1,), (1,)), ((), ())), preferred_element_type=F32
            ).astype(BF16)
            for k in range(all_terms):
                for v in range(nvec):
                    inner[i * rows + v * part:i * rows + (v + 1) * part, k * width:(k + 1) * width] = product[
                        k * part:(k + 1) * part, v * width:(v + 1) * width
                    ]
        total = jnp.dot(
            inner[...], lg[...].reshape(all_terms * width, width), preferred_element_type=F32
        ).astype(BF16)
        sg[j, plane] = total
        for i in range(chunk):
            s = j * chunk + i
            turned[:, s * width:(s + 1) * width] = total[i * rows:(i + 1) * rows]

    def assemble(j):
        for i in range(chunk):
            for v in range(nvec):
                low = i * rows + v * part
                block = sg[j, :, low:low + part].reshape(width, width)
                out[v, j * chunk + i] = block.T

    reductions = []

    def reduce_sends(stage, mine, n, devices):
        for d in range(1, n):
            copy = remote(
                red.at[stage, mine], red.at[stage, mine], red_send.at[stage, d - 1], red_recv.at[stage, d - 1],
                devices[d - 1],
            )
            copy.start()
            reductions.append(copy)

    def reduce_sum(stage, mine, n, devices):
        for d in range(1, n):
            slot = red.at[stage, shift(mine, -d, n)]
            remote(slot, slot, red_send.at[stage, d - 1], red_recv.at[stage, d - 1], devices[d - 1]).wait_recv()
        total = red[stage, 0]
        for i in range(1, n):
            total = total + red[stage, i]
        return total

    stages = [(plane, planes, above), (first, side, along), (second, side, across), (core, 2, [sibling])]

    def subspace_start():
        row = lax.broadcasted_iota(jnp.int32, (rows, width), 0)
        column = lax.broadcasted_iota(jnp.int32, (rows, width), 1)
        own = column == lax.rem(row, part) + plane * part
        tile_row = lax.broadcasted_iota(jnp.int32, red.shape[-2:], 0)
        tile_column = lax.broadcasted_iota(jnp.int32, red.shape[-2:], 1)
        tile = jnp.zeros(red.shape[-2:], F32)
        for i in range(nvec):
            product = jnp.dot(
                turned[...], w[i].reshape(sectors * width, width), preferred_element_type=F32
            )
            product = jnp.where(own, product, 0.0)
            for j in range(nvec):
                value = jnp.sum(product[j * part:(j + 1) * part], axis=(0, 1), keepdims=True)
                tile = tile + jnp.where((tile_row == i) & (tile_column == j), value, 0.0)
        red[0, plane] = tile
        reduce_sends(0, *stages[0])

    def subspace_stage(stage):
        total = reduce_sum(stage, *stages[stage])
        if stage + 1 < len(stages):
            red[stage + 1, stages[stage + 1][0]] = total
            reduce_sends(stage + 1, *stages[stage + 1])
        else:
            sub[...] = total * (1.0 / math.sqrt(2 * side * side * sectors * width * width))

    far = planes // 2
    for t in range(chunks + max(far, 4)):
        if t < chunks:
            compute(t)
            sigma_rings[t].start()
        for j in range(chunks):
            d = t - j
            if 1 <= d <= far:
                sigma_rings[j].step(d)
                if d == far:
                    assemble(j)
            elif planes == 1 and d == 1:
                assemble(j)
        if t == chunks - 1:
            subspace_start()
        elif t >= chunks and t - chunks < len(stages):
            subspace_stage(t - chunks)

    for copy in slices + handed + reductions:
        copy.wait_send()
    for each in [left, one] + two + sigma_rings:
        each.finish()


def body(wavefunction, right_number, left_dim, right_dim, left_ops, right_ops, set_kind, *, chunk=4):
    nvec, sectors, width, _ = wavefunction.shape
    planes = lax.axis_size("ops")
    places = lax.axis_size("sec")
    side = math.isqrt(places // 2)
    terms = left_ops.shape[0]
    part = width // planes
    rows = nvec * part
    chunks = sectors // chunk
    rings = 2 + side + chunks
    vmem = pl.BlockSpec(memory_space=pltpu.VMEM)
    smem = pl.BlockSpec(memory_space=pltpu.SMEM)
    dma = pltpu.SemaphoreType.DMA
    most = max(planes - 1, side - 1, 1)
    out, sub = pl.pallas_call(
        functools.partial(kernel, planes, side, chunk),
        out_shape=(
            jax.ShapeDtypeStruct(wavefunction.shape, BF16),
            jax.ShapeDtypeStruct((8, 128), F32),
        ),
        in_specs=[pl.BlockSpec(memory_space=pl.ANY), smem, smem, smem, vmem, vmem, smem],
        out_specs=(vmem, vmem),
        scratch_shapes=[
            pltpu.VMEM(wavefunction.shape, BF16),
            pltpu.VMEM((planes, terms * part, width), BF16),
            pltpu.VMEM((places, planes * terms * part, width), BF16),
            pltpu.VMEM((planes, terms * width, width), BF16),
            pltpu.VMEM((chunk * rows, planes * terms * width), BF16),
            pltpu.VMEM((chunks, planes, chunk * rows, width), BF16),
            pltpu.VMEM((rows, sectors * width), BF16),
            pltpu.VMEM((4, max(planes, side, 2), 8, 128), F32),
            dma(()),
            dma((max(planes - 1, 1),)),
            dma((max(planes - 1, 1),)),
            dma((rings, max(planes, side))),
            dma((rings, max(planes, side))),
            dma((side * side,)),
            dma((side * side,)),
            dma((4, most)),
            dma((4, most)),
        ],
        compiler_params=pltpu.CompilerParams(
            collective_id=0, has_side_effects=True, vmem_limit_bytes=48 * 1024 * 1024
        ),
        cost_estimate=pl.CostEstimate(
            flops=4 * sectors * nvec * terms * width**3, bytes_accessed=6 * 1024 * 1024, transcendentals=0
        ),
    )(wavefunction, right_number, left_dim, right_dim, left_ops, right_ops, set_kind)
    return out, sub[:nvec, :nvec]


def solution(mesh):
    return jax.shard_map(
        body,
        mesh=mesh,
        in_specs=(
            P(None, "sec", None, None),
            P("sec", None),
            P("sec"),
            P("sec"),
            P("ops", "sec", None, None),
            P("ops", "sec", None, None),
            P("ops"),
        ),
        out_specs=(P(None, "sec", None, None), P()),
        check_vma=False,
    )
```

```python
import functools
import math

import jax
import jax.numpy as jnp
from jax import lax
from jax.experimental import pallas as pl
from jax.experimental.pallas import tpu as pltpu
from jax.sharding import PartitionSpec as P

MESH = pl.DeviceIdType.MESH
BF16 = jnp.bfloat16
F32 = jnp.float32


def remote(src, dst, send, recv, device):
    return pltpu.make_async_remote_copy(
        src_ref=src, dst_ref=dst, send_sem=send, recv_sem=recv, device_id=device, device_id_type=MESH
    )


class Ring:
    def __init__(self, n, me, device, slot, half, send, recv):
        self.n, self.me, self.device = n, me, device
        self.slot, self.half, self.send, self.recv = slot, half, send, recv
        self.sent = []

    def at(self, offset):
        return lax.rem(self.me + (offset + self.n), self.n)

    def ref(self, offset, distance, way):
        if 2 * distance == self.n:
            return self.half(self.at(offset), way)
        return self.slot(self.at(offset))

    def pass_on(self, distance, way):
        step = 1 if way == 0 else -1
        block = self.ref(-step * (distance - 1), distance, way)
        index = way * (self.n // 2) + distance - 1
        copy = remote(block, block, self.send(index), self.recv(index), self.device(self.at(step)))
        copy.start()
        self.sent.append(copy)

    def start(self):
        if self.n > 1:
            self.pass_on(1, 0)
            self.pass_on(1, 1)

    def step(self, distance):
        if 2 * distance > self.n:
            return
        for way in range(2):
            step = 1 if way == 0 else -1
            block = self.ref(-step * distance, distance, way)
            index = way * (self.n // 2) + distance - 1
            remote(block, block, self.send(index), self.recv(index), self.device(self.at(step))).wait_recv()
            if 2 * (distance + 1) <= self.n:
                self.pass_on(distance + 1, way)

    def finish(self):
        for copy in self.sent:
            copy.wait_send()
        self.sent = []


def kernel(
    planes, side, chunk,
    w_hbm, number_hbm, left_dim_hbm, right_dim_hbm, left_hbm, right_hbm, kind_hbm,
    out, sub,
    w, number, left_dim, right_dim, left_ops, right_ops, kind, rt, rg_low, rg_high, lg, inner, sg, turned, red,
    in_sem, a2a_send, a2a_recv, first_send, first_recv, second_send, second_recv,
    ring_send, ring_recv, sib_send, sib_recv, red_send, red_recv,
):
    terms, width = left_ops.shape[0], left_ops.shape[-1]
    nvec, sectors = w.shape[0], w.shape[1]
    part = width // planes // 2
    rows = nvec * part
    span = terms * part
    chunks = sectors // chunk
    all_terms = terms * planes
    plane = lax.axis_index("ops")
    place = lax.axis_index("sec")
    core = lax.rem(place, 2)
    chip = place // 2
    px, py = lax.rem(chip, side), chip // side
    first = px * (1 - core) + py * core
    second = py * (1 - core) + px * core

    def sector_of(one, two, c):
        x = one * (1 - c) + two * c
        y = two * (1 - c) + one * c
        return 2 * (y * side + x) + c

    def shift(base, offset, n):
        return lax.rem(base + (offset + n), n)

    above = [{"ops": shift(plane, d, planes)} for d in range(1, planes)]
    along = [{"sec": sector_of(shift(first, d, side), second, core)} for d in range(1, side)]
    across = [{"sec": sector_of(first, shift(second, d, side), core)} for d in range(1, side)]
    sibling = {"sec": place + 1 - 2 * core}

    barrier = pltpu.get_barrier_semaphore()
    partners = above + along + across + [sibling]
    for device in partners:
        pl.semaphore_signal(barrier, inc=1, device_id=device, device_id_type=MESH)

    loads = [
        pltpu.make_async_copy(a, b, in_sem.at[i])
        for i, (a, b) in enumerate([
            (right_hbm, right_ops), (right_dim_hbm, right_dim), (left_hbm, left_ops), (left_dim_hbm, left_dim),
            (kind_hbm, kind), (number_hbm, number), (w_hbm, w),
        ])
    ]
    for copy in loads:
        copy.start()

    rg = (rg_low, rg_high)
    lane = lax.broadcasted_iota(jnp.int32, (width, width), 1)
    sub_lane = lax.broadcasted_iota(jnp.int32, (width, width), 0)
    loads[0].wait()
    loads[1].wait()
    right_keep = (lane < right_dim[0]) & (sub_lane < right_dim[0])
    blocks = [jnp.where(right_keep, right_ops[k, 0].astype(F32), 0.0).T for k in range(terms)]
    for o in range(planes):
        for h in range(2):
            low = (h * planes + o) * part
            rt[o, h] = jnp.concatenate([block[low:low + part] for block in blocks], axis=0).astype(BF16)

    def slot(r, h, o):
        return rg[h].at[r, pl.ds(pl.multiple_of(o * span, span), span)]

    for h in range(2):
        rg[h][place, pl.ds(pl.multiple_of(plane * span, span), span)] = rt[plane, h]
    for copy in loads[2:5]:
        copy.wait()
    left_keep = (lane < left_dim[0]) & (sub_lane < left_dim[0])
    for k in range(terms):
        block = jnp.where(left_keep, left_ops[k, 0].astype(F32), 0.0)
        normal = (jnp.zeros((width, width), jnp.int32) + kind[k]) == 0
        lg[plane, k * width:(k + 1) * width] = jnp.where(normal, block.T, block).astype(BF16)

    pl.semaphore_wait(barrier, len(partners))
    sends = []

    def send(src, dst, send_sem, recv_sem, device):
        copy = remote(src, dst, send_sem, recv_sem, device)
        copy.start()
        sends.append(copy)

    def arrived(ref, send_sem, recv_sem):
        remote(ref, ref, send_sem, recv_sem, sibling).wait_recv()

    far_first = sorted(range(1, planes), key=lambda d: -min(d, planes - d))
    for h in range(2):
        for d in far_first:
            to = shift(plane, d, planes)
            send(rt.at[to, h], slot(place, h, plane), a2a_send.at[h, d], a2a_recv.at[h, d], {"ops": to})

    rings = [0]

    def ring(slot_of, half_of):
        index = rings[0]
        rings[0] += 1
        return Ring(
            planes, plane, lambda q: {"ops": q}, slot_of, half_of,
            lambda i: ring_send.at[index, i], lambda i: ring_recv.at[index, i],
        )

    pieces = 2
    deep = terms * width // pieces

    def left_ring(i):
        return ring(
            lambda q: lg.at[q, pl.ds(i * deep, deep)],
            lambda q, h: lg.at[q, pl.ds(i * deep + h * (deep // 2), deep // 2)],
        )

    left = [left_ring(i) for i in range(pieces)]

    def left_step(d):
        for each in left:
            each.step(d)

    for each in left:
        each.start()

    order = [d for d in (1, 3, 2) if d < side]

    def block(h, j, d):
        return rg[h].at[sector_of(shift(first, -j, side), shift(second, -d, side), core)]

    def first_sends(h):
        for d in reversed(order):
            send(block(h, 0, 0), block(h, 0, 0), first_send.at[h, d], first_recv.at[h, d], along[d - 1])

    def first_arrival(h, d):
        arrived(block(h, d, 0), first_send.at[h, d], first_recv.at[h, d])

    def second_sends(h, j):
        for d in order:
            send(block(h, j, 0), block(h, j, 0), second_send.at[h, j, d], second_recv.at[h, j, d], across[d - 1])

    def second_arrival(h, j, d):
        arrived(block(h, j, d), second_send.at[h, j, d], second_recv.at[h, j, d])

    def hand(h, j, d):
        send(block(h, j, d), block(h, j, d), sib_send.at[h, j, d], sib_recv.at[h, j, d], sibling)

    def handed(h):
        for j in range(side):
            for d in range(side):
                theirs = rg[h].at[sector_of(shift(second, -j, side), shift(first, -d, side), 1 - core)]
                arrived(theirs, sib_send.at[h, j, d], sib_recv.at[h, j, d])

    for h in range(2):
        for d in reversed(far_first):
            arrived(slot(place, h, shift(plane, -d, planes)), a2a_send.at[h, d], a2a_recv.at[h, d])
        first_sends(h)
        second_sends(h, 0)
        hand(h, 0, 0)
    left_step(1)
    for h in range(2):
        for j in order:
            first_arrival(h, j)
            second_sends(h, j)
            hand(h, j, 0)
        if h == 0:
            left_step(2)

    def second_arrivals(h):
        for j in [0] + order:
            for d in order:
                second_arrival(h, j, d)
                hand(h, j, d)
            if h == 0 and j == 0:
                left_step(3)

    second_arrivals(0)
    left_step(4)
    for copy in loads[5:]:
        copy.wait()
    handed(0)

    def sigma_ring(h, j):
        half = chunk * rows // 2
        return ring(
            lambda q: sg.at[h, j, q], lambda q, way: sg.at[h, j, q, pl.ds(way * half, half)]
        )

    sigma_rings = [[sigma_ring(h, j) for j in range(chunks)] for h in range(2)]

    def compute(h, j):
        for i in range(chunk):
            s = j * chunk + i
            product = lax.dot_general(
                rg[h][number[s]], w[:, s].reshape(nvec * width, width), (((1,), (1,)), ((), ())),
                preferred_element_type=F32,
            ).reshape(all_terms, part, nvec * width)
            product = jnp.concatenate(
                [product[:, :, v * width:(v + 1) * width] for v in range(nvec)], axis=1
            ).astype(BF16)
            for k in range(all_terms):
                inner[i * rows:(i + 1) * rows, k * width:(k + 1) * width] = product[k]
        total = jnp.dot(
            inner[...], lg[...].reshape(all_terms * width, width), preferred_element_type=F32
        ).astype(BF16)
        sg[h, j, plane] = total
        for i in range(chunk):
            s = j * chunk + i
            turned[h * rows:(h + 1) * rows, s * width:(s + 1) * width] = total[i * rows:(i + 1) * rows]
        sigma_rings[h][j].start()

    def sigma_step(h, d):
        for j in range(chunks):
            sigma_rings[h][j].step(d)

    def assemble(j):
        for i in range(chunk):
            halves = [
                sg[h, j, :, i * rows:(i + 1) * rows].astype(F32).reshape(planes, nvec, part, width) for h in range(2)
            ]
            for v in range(nvec):
                joined = jnp.concatenate([half[:, v].reshape(planes * part, width) for half in halves], axis=0)
                out[v, j * chunk + i] = joined.astype(BF16).T

    stages = [(plane, planes, above), (first, side, along), (second, side, across), (core, 2, [sibling])]

    def reduce_sends(stage):
        mine, n, devices = stages[stage]
        for d in range(1, n):
            send(
                red.at[stage, mine], red.at[stage, mine], red_send.at[stage, d], red_recv.at[stage, d], devices[d - 1]
            )

    def subspace_start():
        row = lax.broadcasted_iota(jnp.int32, (2 * rows, width), 0)
        column = lax.broadcasted_iota(jnp.int32, (2 * rows, width), 1)
        own = column == (row // rows * planes + plane) * part + lax.rem(row, part)
        vector = lax.rem(row, rows) // part
        tile_row = lax.broadcasted_iota(jnp.int32, red.shape[-2:], 0)
        tile_column = lax.broadcasted_iota(jnp.int32, red.shape[-2:], 1)
        tile = jnp.zeros(red.shape[-2:], F32)
        for i in range(nvec):
            product = jnp.dot(
                turned[...], w[i].reshape(sectors * width, width), preferred_element_type=F32
            )
            for j in range(nvec):
                value = jnp.sum(jnp.where(own & (vector == j), product, 0.0), axis=(0, 1), keepdims=True)
                tile = tile + jnp.where((tile_row == i) & (tile_column == j), value, 0.0)
        red[0, plane] = tile
        reduce_sends(0)

    def subspace_stage(stage):
        mine, n, _ = stages[stage]
        for d in range(1, n):
            arrived(red.at[stage, shift(mine, -d, n)], red_send.at[stage, d], red_recv.at[stage, d])
        total = red[stage, 0]
        for i in range(1, n):
            total = total + red[stage, i]
        if stage + 1 < len(stages):
            red[stage + 1, stages[stage + 1][0]] = total
            reduce_sends(stage + 1)
        else:
            sub[...] = total * (1.0 / math.sqrt(2 * side * side * sectors * width * width))

    for j in range(chunks):
        compute(0, j)
    second_arrivals(1)
    sigma_step(0, 1)
    handed(1)
    for j in range(chunks):
        compute(1, j)
    sigma_step(0, 2)
    subspace_start()
    sigma_step(1, 1)
    sigma_step(0, 3)
    subspace_stage(0)
    sigma_step(1, 2)
    sigma_step(0, 4)
    subspace_stage(1)
    sigma_step(1, 3)
    subspace_stage(2)
    for j in range(chunks):
        sigma_rings[1][j].step(4)
        assemble(j)
        if j == 0:
            subspace_stage(3)

    for copy in sends:
        copy.wait_send()
    for each in left + sigma_rings[0] + sigma_rings[1]:
        each.finish()


def body(wavefunction, right_number, left_dim, right_dim, left_ops, right_ops, set_kind, *, chunk=8):
    nvec, sectors, width, _ = wavefunction.shape
    planes = lax.axis_size("ops")
    places = lax.axis_size("sec")
    side = math.isqrt(places // 2)
    terms = left_ops.shape[0]
    part = width // planes // 2
    rows = nvec * part
    chunks = sectors // chunk
    vmem = pl.BlockSpec(memory_space=pltpu.VMEM)
    hbm = pl.BlockSpec(memory_space=pltpu.HBM)
    dma = pltpu.SemaphoreType.DMA
    out, sub = pl.pallas_call(
        functools.partial(kernel, planes, side, chunk),
        out_shape=(
            jax.ShapeDtypeStruct(wavefunction.shape, BF16),
            jax.ShapeDtypeStruct((8, 128), F32),
        ),
        in_specs=[hbm] * 7,
        out_specs=(vmem, vmem),
        scratch_shapes=[
            pltpu.VMEM(wavefunction.shape, BF16),
            pltpu.SMEM((sectors,), jnp.int32),
            pltpu.SMEM(left_dim.shape, jnp.int32),
            pltpu.SMEM(right_dim.shape, jnp.int32),
            pltpu.VMEM(left_ops.shape, BF16),
            pltpu.VMEM(right_ops.shape, BF16),
            pltpu.SMEM(set_kind.shape, jnp.int32),
            pltpu.VMEM((planes, 2, terms * part, width), BF16),
            pltpu.VMEM((places, planes * terms * part, width), BF16),
            pltpu.VMEM((places, planes * terms * part, width), BF16),
            pltpu.VMEM((planes, terms * width, width), BF16),
            pltpu.VMEM((chunk * rows, planes * terms * width), BF16),
            pltpu.VMEM((2, chunks, planes, chunk * rows, width), BF16),
            pltpu.VMEM((2 * rows, sectors * width), BF16),
            pltpu.VMEM((4, max(planes, side, 2), 8, 128), F32),
            dma((7,)),
            dma((2, planes)),
            dma((2, planes)),
            dma((2, side)),
            dma((2, side)),
            dma((2, side, side)),
            dma((2, side, side)),
            dma((2 + 2 * chunks, planes)),
            dma((2 + 2 * chunks, planes)),
            dma((2, side, side)),
            dma((2, side, side)),
            dma((4, max(planes, side, 2))),
            dma((4, max(planes, side, 2))),
        ],
        compiler_params=pltpu.CompilerParams(
            collective_id=0, has_side_effects=True, vmem_limit_bytes=60 * 1024 * 1024
        ),
        cost_estimate=pl.CostEstimate(
            flops=4 * sectors * nvec * terms * width**3, bytes_accessed=6 * 1024 * 1024, transcendentals=0
        ),
    )(wavefunction, right_number.reshape(sectors), left_dim, right_dim, left_ops, right_ops, set_kind)
    return out, sub[:nvec, :nvec]


def solution(mesh):
    return jax.shard_map(
        body,
        mesh=mesh,
        in_specs=(
            P(None, "sec", None, None),
            P("sec", None),
            P("sec"),
            P("sec"),
            P("ops", "sec", None, None),
            P("ops", "sec", None, None),
            P("ops"),
        ),
        out_specs=(P(None, "sec", None, None), P()),
        check_vma=False,
    )
```

```python
import functools
import math

import jax
import jax.numpy as jnp
from jax import lax
from jax.experimental import pallas as pl
from jax.experimental.pallas import tpu as pltpu
from jax.sharding import PartitionSpec as P

MESH = pl.DeviceIdType.MESH
BF16 = jnp.bfloat16
F32 = jnp.float32


def remote(src, dst, send, recv, device):
    return pltpu.make_async_remote_copy(
        src_ref=src, dst_ref=dst, send_sem=send, recv_sem=recv, device_id=device, device_id_type=MESH
    )


class Ring:
    def __init__(self, n, me, device, slot, half, send, recv):
        self.n, self.me, self.device = n, me, device
        self.slot, self.half, self.send, self.recv = slot, half, send, recv

    def at(self, offset):
        return lax.rem(self.me + (offset + self.n), self.n)

    def ref(self, offset, distance, way):
        if 2 * distance == self.n:
            return self.half(self.at(offset), way)
        return self.slot(self.at(offset))

    def copy(self, offset, distance, way):
        block = self.ref(offset, distance, way)
        index = way * (self.n // 2) + distance - 1
        return remote(block, block, self.send, self.recv(index), self.device(self.at(1 if way == 0 else -1)))

    def pass_on(self, distance, way):
        step = 1 if way == 0 else -1
        self.copy(-step * (distance - 1), distance, way).start()

    def start(self):
        if self.n > 1:
            self.pass_on(1, 0)
            self.pass_on(1, 1)

    def step(self, distance):
        if 2 * distance > self.n:
            return
        for way in range(2):
            self.copy(-distance if way == 0 else distance, distance, way).wait_recv()
            if 2 * (distance + 1) <= self.n:
                self.pass_on(distance + 1, way)


def kernel(
    planes, side, chunk,
    left_dim, right_dim, w_hbm, number_hbm, kind_hbm, left_hbm, right_hbm,
    out, sub,
    w, number, kind, left_ops, right_ops, rt, rg_low, rg_high, lg, inner, sg, picked, red,
    in_sem, a2a_send, a2a_recv, first_send, first_recv, second_send, second_recv,
    left_send, left_recv, sigma_send, sigma_recv, sib_send, sib_recv, red_send, red_recv,
):
    rg = (rg_low, rg_high)
    terms, width = left_ops.shape[0], left_ops.shape[-1]
    nvec, sectors = w.shape[0], w.shape[1]
    part = width // planes // 2
    rows = nvec * part
    span = terms * part
    chunks = sectors // chunk
    all_terms = terms * planes
    plane = lax.axis_index("ops")
    place = lax.axis_index("sec")
    core = lax.rem(place, 2)
    chip = place // 2
    px, py = lax.rem(chip, side), chip // side
    first = px * (1 - core) + py * core
    second = py * (1 - core) + px * core

    def sector_of(one, two):
        x = one * (1 - core) + two * core
        y = two * (1 - core) + one * core
        return 2 * (y * side + x) + core

    def shift(base, offset, n):
        return lax.rem(base + (offset + n), n)

    above = [{"ops": shift(plane, d, planes)} for d in range(1, planes)]
    along = [{"sec": sector_of(shift(first, d, side), second)} for d in range(1, side)]
    across = [{"sec": sector_of(first, shift(second, d, side))} for d in range(1, side)]
    sibling = {"sec": place + 1 - 2 * core}

    barrier = pltpu.get_barrier_semaphore()
    partners = above + along + across + [sibling]
    for device in partners:
        pl.semaphore_signal(barrier, inc=1, device_id=device, device_id_type=MESH)

    loads = [
        pltpu.make_async_copy(a, b, in_sem.at[i])
        for i, (a, b) in enumerate([
            (right_hbm, right_ops), (kind_hbm, kind), (left_hbm, left_ops), (number_hbm, number), (w_hbm, w)
        ])
    ]
    for copy in loads:
        copy.start()

    lane = lax.broadcasted_iota(jnp.int32, (width, width), 1)
    sub_lane = lax.broadcasted_iota(jnp.int32, (width, width), 0)
    loads[0].wait()
    right_keep = (lane < right_dim[0]) & (sub_lane < right_dim[0])
    blocks = [jnp.where(right_keep, right_ops[k, 0].astype(F32), 0.0).T for k in range(terms)]
    for o in range(planes):
        for h in range(2):
            low = (h * planes + o) * part
            rt[h, o] = jnp.concatenate([block[low:low + part] for block in blocks], axis=0).astype(BF16)

    def at(c, one, two):
        return (c * side + one) * side + two

    mine = at(core, first, second)

    def slot(h, o):
        return rg[h].at[mine, pl.ds(pl.multiple_of(o * span, span), span)]

    for h in range(2):
        rg[h][mine, pl.ds(pl.multiple_of(plane * span, span), span)] = rt[h, plane]
    for copy in loads[1:3]:
        copy.wait()
    left_keep = (lane < left_dim[0]) & (sub_lane < left_dim[0])
    for k in range(terms):
        block = jnp.where(left_keep, left_ops[k, 0].astype(F32), 0.0)
        normal = (jnp.zeros((width, width), jnp.int32) + kind[k]) == 0
        lg[plane, k * width:(k + 1) * width] = jnp.where(normal, block.T, block).astype(BF16)

    pl.semaphore_wait(barrier, len(partners))

    def wait_for(ref, semaphore):
        remote(ref, ref, semaphore, semaphore, sibling).wait_recv()

    far_first = sorted(range(1, planes), key=lambda d: -min(d, planes - d))
    for h in range(2):
        for d in far_first:
            to = shift(plane, d, planes)
            remote(rt.at[h, to], slot(h, plane), a2a_send.at[h], a2a_recv.at[h], {"ops": to}).start()

    pieces = 2
    deep = terms * width // pieces

    def left_ring(i):
        return Ring(
            planes, plane, lambda q: {"ops": q},
            lambda q: lg.at[q, pl.ds(i * deep, deep)],
            lambda q, h: lg.at[q, pl.ds(i * deep + h * (deep // 2), deep // 2)],
            left_send.at[0], lambda index: left_recv.at[i, index],
        )

    left = [left_ring(i) for i in range(pieces)]

    def left_step(d):
        for each in left:
            each.step(d)

    for each in left:
        each.start()

    order = [d for d in (1, 3, 2) if d < side]

    def first_sends(h):
        block = rg[h].at[mine]
        for d in reversed(order):
            remote(block, block, first_send.at[h], first_recv.at[h, d], along[d - 1]).start()

    def second_sends(h, j):
        block = rg[h].at[at(core, shift(first, -j, side), second)]
        for d in order:
            remote(block, block, second_send.at[h], second_recv.at[h, j], across[d - 1]).start()

    def line_arrival(h, j):
        wait_for(rg[h].at[pl.ds(0, side - 1)], second_recv.at[h, j])
        line = rg[h].at[pl.ds(at(core, shift(first, -j, side), 0), side)]
        remote(line, line, sib_send.at[h], sib_recv.at[h], sibling).start()

    for h in range(2):
        wait_for(rt.at[h, pl.ds(0, planes - 1)], a2a_recv.at[h])
        first_sends(h)
        second_sends(h, 0)
    left_step(1)
    for h in range(2):
        for j in order:
            wait_for(rg[h].at[0], first_recv.at[h, j])
            second_sends(h, j)
        if h == 0:
            left_step(2)

    for copy in loads[3:]:
        copy.wait()
    pick_row = lax.broadcasted_iota(jnp.int32, (2 * part, width), 0)
    pick_lane = lax.broadcasted_iota(jnp.int32, (2 * part, width), 1)
    pick = jnp.where(
        pick_lane == (pick_row // part * planes + plane) * part + lax.rem(pick_row, part), 1.0, 0.0
    ).astype(BF16)

    def pick_sectors(low, high):
        for s in range(low, high):
            picked[s] = lax.dot_general(
                pick, w[:, s].reshape(nvec * width, width), (((1,), (1,)), ((), ())), preferred_element_type=F32
            )

    pick_sectors(0, sectors // 2)
    line_arrival(0, 0)
    left_step(3)
    pick_sectors(sectors // 2, sectors)
    for j in order:
        line_arrival(0, j)
    left_step(4)
    half_blocks = side * side
    wait_for(rg[0].at[pl.ds(0, half_blocks)], sib_recv.at[0])

    def sigma_ring(h, j):
        half = chunk * rows // 2
        return Ring(
            planes, plane, lambda q: {"ops": q},
            lambda q: sg.at[h, j, q], lambda q, way: sg.at[h, j, q, pl.ds(way * half, half)],
            sigma_send.at[0], lambda index: sigma_recv.at[h, j, index],
        )

    sigma_rings = [[sigma_ring(h, j) for j in range(chunks)] for h in range(2)]
    traces = [[jnp.zeros((part, width), F32) for _ in range(nvec)] for _ in range(nvec)]

    def right_of(s):
        r = number[s]
        c = lax.rem(r, 2)
        x, y = lax.rem(r // 2, side), r // 2 // side
        return at(c, x * (1 - c) + y * c, y * (1 - c) + x * c)

    def compute(h, j):
        for i in range(chunk):
            s = j * chunk + i
            product = lax.dot_general(
                rg[h][right_of(s)], w[:, s].reshape(nvec * width, width), (((1,), (1,)), ((), ())),
                preferred_element_type=F32,
            ).reshape(all_terms, part, nvec * width)
            product = jnp.concatenate(
                [product[:, :, v * width:(v + 1) * width] for v in range(nvec)], axis=1
            ).astype(BF16)
            for k in range(all_terms):
                inner[i * rows:(i + 1) * rows, k * width:(k + 1) * width] = product[k]
        total = jnp.dot(
            inner[...], lg[...].reshape(all_terms * width, width), preferred_element_type=F32
        ).astype(BF16)
        sg[h, j, plane] = total
        sigma_rings[h][j].start()
        total = total.astype(F32).reshape(chunk, nvec, part, width)
        for i in range(nvec):
            other = picked[j * chunk:(j + 1) * chunk, h * part:(h + 1) * part, i * width:(i + 1) * width]
            for v in range(nvec):
                traces[i][v] = traces[i][v] + jnp.sum(other * total[:, v], axis=0)

    def sigma_step(h, d):
        for j in range(chunks):
            sigma_rings[h][j].step(d)

    def assemble(j):
        for i in range(chunk):
            halves = [
                sg[h, j, :, i * rows:(i + 1) * rows].astype(F32).reshape(planes, nvec, part, width) for h in range(2)
            ]
            for v in range(nvec):
                joined = jnp.concatenate([half[:, v].reshape(planes * part, width) for half in halves], axis=0)
                out[v, j * chunk + i] = joined.astype(BF16).T

    stages = [(plane, planes, above), (first, side, along), (second, side, across), (core, 2, [sibling])]

    def reduce_sends(stage):
        me, n, devices = stages[stage]
        for d in range(1, n):
            remote(
                red.at[stage, me], red.at[stage, me], red_send.at[stage], red_recv.at[stage], devices[d - 1]
            ).start()

    def subspace_start():
        tile_row = lax.broadcasted_iota(jnp.int32, red.shape[-2:], 0)
        tile_column = lax.broadcasted_iota(jnp.int32, red.shape[-2:], 1)
        tile = jnp.zeros(red.shape[-2:], F32)
        for i in range(nvec):
            for v in range(nvec):
                value = jnp.sum(traces[i][v], axis=(0, 1), keepdims=True)
                tile = tile + jnp.where((tile_row == i) & (tile_column == v), value, 0.0)
        red[0, plane] = tile
        reduce_sends(0)

    def subspace_stage(stage):
        _, n, _ = stages[stage]
        wait_for(red.at[stage, pl.ds(0, n - 1)], red_recv.at[stage])
        total = red[stage, 0]
        for i in range(1, n):
            total = total + red[stage, i]
        if stage + 1 < len(stages):
            red[stage + 1, stages[stage + 1][0]] = total
            reduce_sends(stage + 1)
        else:
            sub[...] = total * (1.0 / math.sqrt(2 * side * side * sectors * width * width))

    for j in range(chunks):
        compute(0, j)
    for j in [0] + order:
        line_arrival(1, j)
    sigma_step(0, 1)
    wait_for(rg[1].at[pl.ds(0, half_blocks)], sib_recv.at[1])
    for j in range(chunks):
        compute(1, j)
    subspace_start()
    sigma_step(0, 2)
    sigma_step(1, 1)
    sigma_step(0, 3)
    subspace_stage(0)
    sigma_step(1, 2)
    sigma_step(0, 4)
    subspace_stage(1)
    sigma_step(1, 3)
    subspace_stage(2)

    for h in range(2):
        wait_for(rt.at[h, pl.ds(0, planes - 1)], a2a_send.at[h])
        wait_for(rg[h].at[pl.ds(0, side - 1)], first_send.at[h])
        wait_for(rg[h].at[pl.ds(0, side * (side - 1))], second_send.at[h])
        wait_for(rg[h].at[pl.ds(0, half_blocks)], sib_send.at[h])
    wait_for(lg.at[pl.ds(0, planes - 1)], left_send.at[0])
    for j in range(chunks):
        sigma_rings[1][j].step(4)
        assemble(j)
        if j == 0:
            subspace_stage(3)
    wait_for(sg.at[:, :, pl.ds(0, planes - 1)], sigma_send.at[0])
    for stage, (_, n, _) in enumerate(stages):
        wait_for(red.at[stage, pl.ds(0, n - 1)], red_send.at[stage])


def body(wavefunction, right_number, left_dim, right_dim, left_ops, right_ops, set_kind, *, chunk=16):
    nvec, sectors, width, _ = wavefunction.shape
    planes = lax.axis_size("ops")
    places = lax.axis_size("sec")
    side = math.isqrt(places // 2)
    terms = left_ops.shape[0]
    part = width // planes // 2
    rows = nvec * part
    chunks = sectors // chunk
    vmem = pl.BlockSpec(memory_space=pltpu.VMEM)
    smem = pl.BlockSpec(memory_space=pltpu.SMEM)
    hbm = pl.BlockSpec(memory_space=pltpu.HBM)
    dma = pltpu.SemaphoreType.DMA
    out, sub = pl.pallas_call(
        functools.partial(kernel, planes, side, chunk),
        out_shape=(
            jax.ShapeDtypeStruct(wavefunction.shape, BF16),
            jax.ShapeDtypeStruct((8, 128), F32),
        ),
        in_specs=[smem] * 2 + [hbm] * 5,
        out_specs=(vmem, vmem),
        scratch_shapes=[
            pltpu.VMEM(wavefunction.shape, BF16),
            pltpu.SMEM((sectors,), jnp.int32),
            pltpu.SMEM(set_kind.shape, jnp.int32),
            pltpu.VMEM(left_ops.shape, BF16),
            pltpu.VMEM(right_ops.shape, BF16),
            pltpu.VMEM((2, planes, terms * part, width), BF16),
            pltpu.VMEM((places, planes * terms * part, width), BF16),
            pltpu.VMEM((places, planes * terms * part, width), BF16),
            pltpu.VMEM((planes, terms * width, width), BF16),
            pltpu.VMEM((chunk * rows, planes * terms * width), BF16),
            pltpu.VMEM((2, chunks, planes, chunk * rows, width), BF16),
            pltpu.VMEM((sectors, 2 * part, nvec * width), F32),
            pltpu.VMEM((4, max(planes, side, 2), 8, 128), F32),
            dma((5,)),
            dma((2,)),
            dma((2,)),
            dma((2,)),
            dma((2, side)),
            dma((2,)),
            dma((2, side)),
            dma((1,)),
            dma((2, planes)),
            dma((1,)),
            dma((2, chunks, planes)),
            dma((2,)),
            dma((2,)),
            dma((4,)),
            dma((4,)),
        ],
        compiler_params=pltpu.CompilerParams(
            collective_id=0, has_side_effects=True, vmem_limit_bytes=48 * 1024 * 1024
        ),
        cost_estimate=pl.CostEstimate(
            flops=4 * sectors * nvec * terms * width**3, bytes_accessed=6 * 1024 * 1024, transcendentals=0
        ),
    )(left_dim, right_dim, *[
        pltpu.with_memory_space_constraint(each, pltpu.HBM)
        for each in (
            wavefunction, right_number.reshape(sectors), set_kind, left_ops, right_ops
        )
    ])
    return out, sub[:nvec, :nvec]


def solution(mesh):
    return jax.shard_map(
        body,
        mesh=mesh,
        in_specs=(
            P(None, "sec", None, None),
            P("sec", None),
            P("sec"),
            P("sec"),
            P("ops", "sec", None, None),
            P("ops", "sec", None, None),
            P("ops"),
        ),
        out_specs=(P(None, "sec", None, None), P()),
        check_vma=False,
    )
```

```python
import functools
import math

import jax
import jax.numpy as jnp
from jax import lax
from jax.experimental import pallas as pl
from jax.experimental.pallas import tpu as pltpu
from jax.sharding import PartitionSpec as P

MESH = pl.DeviceIdType.MESH
BF16 = jnp.bfloat16
F32 = jnp.float32


def remote(src, dst, send, recv, device):
    return pltpu.make_async_remote_copy(
        src_ref=src, dst_ref=dst, send_sem=send, recv_sem=recv, device_id=device, device_id_type=MESH
    )


class Ring:
    def __init__(self, n, me, device, slot, half, send, recv):
        self.n, self.me, self.device = n, me, device
        self.slot, self.half, self.send, self.recv = slot, half, send, recv

    def at(self, offset):
        return lax.rem(self.me + (offset + self.n), self.n)

    def ref(self, offset, distance, way):
        if 2 * distance == self.n:
            return self.half(self.at(offset), way)
        return self.slot(self.at(offset))

    def copy(self, offset, distance, way):
        block = self.ref(offset, distance, way)
        index = way * (self.n // 2) + distance - 1
        return remote(block, block, self.send, self.recv(index), self.device(self.at(1 if way == 0 else -1)))

    def pass_on(self, distance, way):
        step = 1 if way == 0 else -1
        self.copy(-step * (distance - 1), distance, way).start()

    def start(self):
        if self.n > 1:
            self.pass_on(1, 0)
            self.pass_on(1, 1)

    def step(self, distance):
        if 2 * distance > self.n:
            return
        for way in range(2):
            self.copy(-distance if way == 0 else distance, distance, way).wait_recv()
            if 2 * (distance + 1) <= self.n:
                self.pass_on(distance + 1, way)


def kernel(
    planes, side, chunk,
    left_dim, right_dim, w_hbm, number_hbm, kind_hbm, left_hbm, right_hbm,
    out, sub,
    w, number, kind, left_ops, right_ops, rt, rg_low, rg_high, lg, inner, sg, picked, red,
    in_sem, a2a_send, a2a_recv, first_send, first_recv, second_send, second_recv,
    left_send, left_recv, sigma_send, sigma_recv, sib_send, sib_recv, red_send, red_recv,
):
    rg = (rg_low, rg_high)
    terms, width = left_ops.shape[0], left_ops.shape[-1]
    nvec, sectors = w.shape[0], w.shape[1]
    part = width // planes // 2
    rows = nvec * part
    span = terms * part
    chunks = sectors // chunk
    all_terms = terms * planes
    plane = lax.axis_index("ops")
    place = lax.axis_index("sec")
    core = lax.rem(place, 2)
    chip = place // 2
    px, py = lax.rem(chip, side), chip // side
    first = px * (1 - core) + py * core
    second = py * (1 - core) + px * core

    def sector_of(one, two):
        x = one * (1 - core) + two * core
        y = two * (1 - core) + one * core
        return 2 * (y * side + x) + core

    def shift(base, offset, n):
        return lax.rem(base + (offset + n), n)

    above = [{"ops": shift(plane, d, planes)} for d in range(1, planes)]
    along = [{"sec": sector_of(shift(first, d, side), second)} for d in range(1, side)]
    across = [{"sec": sector_of(first, shift(second, d, side))} for d in range(1, side)]
    sibling = {"sec": place + 1 - 2 * core}

    barrier = pltpu.get_barrier_semaphore()
    partners = above + along + across + [sibling]
    for device in partners:
        pl.semaphore_signal(barrier, inc=1, device_id=device, device_id_type=MESH)

    loads = [
        pltpu.make_async_copy(a, b, in_sem.at[i])
        for i, (a, b) in enumerate([
            (right_hbm, right_ops), (kind_hbm, kind), (left_hbm, left_ops), (number_hbm, number), (w_hbm, w)
        ])
    ]
    for copy in loads:
        copy.start()

    lane = lax.broadcasted_iota(jnp.int32, (width, width), 1)
    sub_lane = lax.broadcasted_iota(jnp.int32, (width, width), 0)
    loads[0].wait()
    right_keep = (lane < right_dim[0]) & (sub_lane < right_dim[0])
    blocks = [jnp.where(right_keep, right_ops[k, 0].astype(F32), 0.0).T for k in range(terms)]
    for o in range(planes):
        for h in range(2):
            low = (h * planes + o) * part
            rt[h, o] = jnp.concatenate([block[low:low + part] for block in blocks], axis=0).astype(BF16)

    def at(c, one, two):
        return (c * side + one) * side + two

    mine = at(core, first, second)

    def slot(h, o):
        return rg[h].at[mine, pl.ds(pl.multiple_of(o * span, span), span)]

    for h in range(2):
        rg[h][mine, pl.ds(pl.multiple_of(plane * span, span), span)] = rt[h, plane]

    pl.semaphore_wait(barrier, len(partners))

    def wait_for(ref, semaphore):
        remote(ref, ref, semaphore, semaphore, sibling).wait_recv()

    far_first = sorted(range(1, planes), key=lambda d: -min(d, planes - d))
    def slices(h):
        for d in far_first:
            to = shift(plane, d, planes)
            remote(rt.at[h, to], slot(h, plane), a2a_send.at[h], a2a_recv.at[h], {"ops": to}).start()

    slices(0)
    for copy in loads[1:3]:
        copy.wait()
    left_keep = (lane < left_dim[0]) & (sub_lane < left_dim[0])
    for k in range(terms):
        block = jnp.where(left_keep, left_ops[k, 0].astype(F32), 0.0)
        normal = (jnp.zeros((width, width), jnp.int32) + kind[k]) == 0
        lg[plane, k * width:(k + 1) * width] = jnp.where(normal, block.T, block).astype(BF16)

    slices(1)

    pieces = 2
    deep = terms * width // pieces

    def left_ring(i):
        return Ring(
            planes, plane, lambda q: {"ops": q},
            lambda q: lg.at[q, pl.ds(i * deep, deep)],
            lambda q, h: lg.at[q, pl.ds(i * deep + h * (deep // 2), deep // 2)],
            left_send.at[0], lambda index: left_recv.at[i, index],
        )

    left = [left_ring(i) for i in range(pieces)]

    def left_step(d):
        for each in left:
            each.step(d)

    for each in left:
        each.start()

    order = [d for d in (1, 3, 2) if d < side]

    def first_sends(h):
        block = rg[h].at[mine]
        for d in reversed(order):
            remote(block, block, first_send.at[h], first_recv.at[h, d], along[d - 1]).start()

    def second_sends(h, j):
        block = rg[h].at[at(core, shift(first, -j, side), second)]
        for d in order:
            remote(block, block, second_send.at[h], second_recv.at[h, j], across[d - 1]).start()

    def line_arrival(h, j):
        wait_for(rg[h].at[pl.ds(0, side - 1)], second_recv.at[h, j])
        line = rg[h].at[pl.ds(at(core, shift(first, -j, side), 0), side)]
        remote(line, line, sib_send.at[h], sib_recv.at[h], sibling).start()

    for copy in loads[3:]:
        copy.wait()
    pick_row = lax.broadcasted_iota(jnp.int32, (2 * part, width), 0)
    pick_lane = lax.broadcasted_iota(jnp.int32, (2 * part, width), 1)
    pick = jnp.where(
        pick_lane == (pick_row // part * planes + plane) * part + lax.rem(pick_row, part), 1.0, 0.0
    ).astype(BF16)

    def pick_sectors(low, high):
        for s in range(low, high):
            picked[s] = lax.dot_general(
                pick, w[:, s].reshape(nvec * width, width), (((1,), (1,)), ((), ())), preferred_element_type=F32
            )

    def first_arrivals(h):
        for j in order:
            wait_for(rg[h].at[0], first_recv.at[h, j])
            second_sends(h, j)

    pick_sectors(0, 8)
    wait_for(rt.at[0, pl.ds(0, planes - 1)], a2a_recv.at[0])
    first_sends(0)
    pick_sectors(8, 16)
    second_sends(0, 0)
    wait_for(rt.at[1, pl.ds(0, planes - 1)], a2a_recv.at[1])
    first_sends(1)
    left_step(1)
    first_arrivals(0)
    second_sends(1, 0)
    left_step(2)
    first_arrivals(1)
    line_arrival(0, 0)
    left_step(3)
    pick_sectors(16, sectors)
    for j in order:
        line_arrival(0, j)
    left_step(4)
    half_blocks = side * side
    wait_for(rg[0].at[pl.ds(0, half_blocks)], sib_recv.at[0])

    def sigma_ring(h, j):
        half = chunk * rows // 2
        return Ring(
            planes, plane, lambda q: {"ops": q},
            lambda q: sg.at[h, j, q], lambda q, way: sg.at[h, j, q, pl.ds(way * half, half)],
            sigma_send.at[0], lambda index: sigma_recv.at[h, j, index],
        )

    sigma_rings = [[sigma_ring(h, j) for j in range(chunks)] for h in range(2)]
    traces = [[jnp.zeros((part, width), F32) for _ in range(nvec)] for _ in range(nvec)]

    def right_of(s):
        r = number[s]
        c = lax.rem(r, 2)
        x, y = lax.rem(r // 2, side), r // 2 // side
        return at(c, x * (1 - c) + y * c, y * (1 - c) + x * c)

    def compute(h, j):
        for i in range(chunk):
            s = j * chunk + i
            product = lax.dot_general(
                rg[h][right_of(s)], w[:, s].reshape(nvec * width, width), (((1,), (1,)), ((), ())),
                preferred_element_type=F32,
            ).reshape(all_terms, part, nvec * width)
            product = jnp.concatenate(
                [product[:, :, v * width:(v + 1) * width] for v in range(nvec)], axis=1
            ).astype(BF16)
            for k in range(all_terms):
                inner[i * rows:(i + 1) * rows, k * width:(k + 1) * width] = product[k]
        total = jnp.dot(
            inner[...], lg[...].reshape(all_terms * width, width), preferred_element_type=F32
        ).astype(BF16)
        sg[h, j, plane] = total
        sigma_rings[h][j].start()

    def trace(h, j):
        total = sg[h, j, plane].astype(F32).reshape(chunk, nvec, part, width)
        for i in range(nvec):
            other = picked[j * chunk:(j + 1) * chunk, h * part:(h + 1) * part, i * width:(i + 1) * width]
            for v in range(nvec):
                traces[i][v] = traces[i][v] + jnp.sum(other * total[:, v], axis=0)

    def sigma_step(h, d):
        for j in range(chunks):
            sigma_rings[h][j].step(d)

    def assemble(j):
        for i in range(chunk):
            halves = [
                sg[h, j, :, i * rows:(i + 1) * rows].astype(F32).reshape(planes, nvec, part, width) for h in range(2)
            ]
            for v in range(nvec):
                joined = jnp.concatenate([half[:, v].reshape(planes * part, width) for half in halves], axis=0)
                out[v, j * chunk + i] = joined.astype(BF16).T

    stages = [(plane, planes, above), (first, side, along), (second, side, across), (core, 2, [sibling])]

    def reduce_sends(stage):
        me, n, devices = stages[stage]
        for d in range(1, n):
            remote(
                red.at[stage, me], red.at[stage, me], red_send.at[stage], red_recv.at[stage], devices[d - 1]
            ).start()

    def subspace_start():
        tile_row = lax.broadcasted_iota(jnp.int32, red.shape[-2:], 0)
        tile_column = lax.broadcasted_iota(jnp.int32, red.shape[-2:], 1)
        tile = jnp.zeros(red.shape[-2:], F32)
        for i in range(nvec):
            for v in range(nvec):
                value = jnp.sum(traces[i][v], axis=(0, 1), keepdims=True)
                tile = tile + jnp.where((tile_row == i) & (tile_column == v), value, 0.0)
        red[0, plane] = tile
        reduce_sends(0)

    def subspace_stage(stage):
        _, n, _ = stages[stage]
        wait_for(red.at[stage, pl.ds(0, n - 1)], red_recv.at[stage])
        total = red[stage, 0]
        for i in range(1, n):
            total = total + red[stage, i]
        if stage + 1 < len(stages):
            red[stage + 1, stages[stage + 1][0]] = total
            reduce_sends(stage + 1)
        else:
            sub[...] = total * (1.0 / math.sqrt(2 * side * side * sectors * width * width))

    for j in range(chunks):
        compute(0, j)
    for j in range(chunks):
        trace(0, j)
    for j in [0] + order:
        line_arrival(1, j)
    sigma_step(0, 1)
    wait_for(rg[1].at[pl.ds(0, half_blocks)], sib_recv.at[1])
    for j in range(chunks):
        compute(1, j)
    for j in range(chunks):
        trace(1, j)
    subspace_start()
    sigma_step(0, 2)
    sigma_step(1, 1)
    sigma_step(0, 3)
    subspace_stage(0)
    sigma_step(1, 2)
    sigma_step(0, 4)
    subspace_stage(1)
    sigma_step(1, 3)
    subspace_stage(2)

    for h in range(2):
        wait_for(rt.at[h, pl.ds(0, planes - 1)], a2a_send.at[h])
        wait_for(rg[h].at[pl.ds(0, side - 1)], first_send.at[h])
        wait_for(rg[h].at[pl.ds(0, side * (side - 1))], second_send.at[h])
        wait_for(rg[h].at[pl.ds(0, half_blocks)], sib_send.at[h])
    wait_for(lg.at[pl.ds(0, planes - 1)], left_send.at[0])
    for j in range(chunks):
        sigma_rings[1][j].step(4)
        assemble(j)
        if j == 0:
            subspace_stage(3)
    wait_for(sg.at[:, :, pl.ds(0, planes - 1)], sigma_send.at[0])
    for stage, (_, n, _) in enumerate(stages):
        wait_for(red.at[stage, pl.ds(0, n - 1)], red_send.at[stage])


def body(wavefunction, right_number, left_dim, right_dim, left_ops, right_ops, set_kind, *, chunk=16):
    nvec, sectors, width, _ = wavefunction.shape
    planes = lax.axis_size("ops")
    places = lax.axis_size("sec")
    side = math.isqrt(places // 2)
    terms = left_ops.shape[0]
    part = width // planes // 2
    rows = nvec * part
    chunks = sectors // chunk
    vmem = pl.BlockSpec(memory_space=pltpu.VMEM)
    smem = pl.BlockSpec(memory_space=pltpu.SMEM)
    hbm = pl.BlockSpec(memory_space=pltpu.HBM)
    dma = pltpu.SemaphoreType.DMA
    out, sub = pl.pallas_call(
        functools.partial(kernel, planes, side, chunk),
        out_shape=(
            jax.ShapeDtypeStruct(wavefunction.shape, BF16),
            jax.ShapeDtypeStruct((8, 128), F32),
        ),
        in_specs=[smem] * 2 + [hbm] * 5,
        out_specs=(vmem, vmem),
        scratch_shapes=[
            pltpu.VMEM(wavefunction.shape, BF16),
            pltpu.SMEM((sectors,), jnp.int32),
            pltpu.SMEM(set_kind.shape, jnp.int32),
            pltpu.VMEM(left_ops.shape, BF16),
            pltpu.VMEM(right_ops.shape, BF16),
            pltpu.VMEM((2, planes, terms * part, width), BF16),
            pltpu.VMEM((places, planes * terms * part, width), BF16),
            pltpu.VMEM((places, planes * terms * part, width), BF16),
            pltpu.VMEM((planes, terms * width, width), BF16),
            pltpu.VMEM((chunk * rows, planes * terms * width), BF16),
            pltpu.VMEM((2, chunks, planes, chunk * rows, width), BF16),
            pltpu.VMEM((sectors, 2 * part, nvec * width), F32),
            pltpu.VMEM((4, max(planes, side, 2), 8, 128), F32),
            dma((5,)),
            dma((2,)),
            dma((2,)),
            dma((2,)),
            dma((2, side)),
            dma((2,)),
            dma((2, side)),
            dma((1,)),
            dma((2, planes)),
            dma((1,)),
            dma((2, chunks, planes)),
            dma((2,)),
            dma((2,)),
            dma((4,)),
            dma((4,)),
        ],
        compiler_params=pltpu.CompilerParams(
            collective_id=0, has_side_effects=True, vmem_limit_bytes=48 * 1024 * 1024
        ),
        cost_estimate=pl.CostEstimate(
            flops=4 * sectors * nvec * terms * width**3, bytes_accessed=6 * 1024 * 1024, transcendentals=0
        ),
    )(left_dim, right_dim, *[
        pltpu.with_memory_space_constraint(each, pltpu.HBM)
        for each in (
            wavefunction, right_number.reshape(sectors), set_kind, left_ops, right_ops
        )
    ])
    return out, sub[:nvec, :nvec]


def solution(mesh):
    return jax.shard_map(
        body,
        mesh=mesh,
        in_specs=(
            P(None, "sec", None, None),
            P("sec", None),
            P("sec"),
            P("sec"),
            P("ops", "sec", None, None),
            P("ops", "sec", None, None),
            P("ops"),
        ),
        out_specs=(P(None, "sec", None, None), P()),
        check_vma=False,
    )
```

```python
import functools
import math

import jax
import jax.numpy as jnp
from jax import lax
from jax.experimental import pallas as pl
from jax.experimental.pallas import tpu as pltpu
from jax.sharding import PartitionSpec as P

MESH = pl.DeviceIdType.MESH
BF16 = jnp.bfloat16
F32 = jnp.float32


def remote(src, dst, send, recv, device):
    return pltpu.make_async_remote_copy(
        src_ref=src, dst_ref=dst, send_sem=send, recv_sem=recv, device_id=device, device_id_type=MESH
    )


class Ring:
    def __init__(self, n, me, device, slot, half, send, recv):
        self.n, self.me, self.device = n, me, device
        self.slot, self.half, self.send, self.recv = slot, half, send, recv

    def at(self, offset):
        return lax.rem(self.me + (offset + self.n), self.n)

    def ref(self, offset, distance, way):
        if 2 * distance == self.n:
            return self.half(self.at(offset), way)
        return self.slot(self.at(offset))

    def copy(self, offset, distance, way):
        block = self.ref(offset, distance, way)
        index = way * (self.n // 2) + distance - 1
        return remote(block, block, self.send, self.recv(index), self.device(self.at(1 if way == 0 else -1)))

    def pass_on(self, distance, way):
        step = 1 if way == 0 else -1
        self.copy(-step * (distance - 1), distance, way).start()

    def start(self):
        if self.n > 1:
            self.pass_on(1, 0)
            self.pass_on(1, 1)

    def step(self, distance):
        if 2 * distance > self.n:
            return
        for way in range(2):
            self.copy(-distance if way == 0 else distance, distance, way).wait_recv()
            if 2 * (distance + 1) <= self.n:
                self.pass_on(distance + 1, way)


def kernel(
    planes, side, chunk,
    left_dim, right_dim, w_hbm, number_hbm, kind_hbm, left_hbm, right_hbm,
    out, sub,
    w, number, kind, left_ops, right_ops, rt, rg_low, rg_high, lg, inner, sg, picked, red,
    in_sem, a2a_send, a2a_recv, first_send, first_recv, second_send, second_recv,
    left_send, left_recv, sigma_send, sigma_recv, sib_send, sib_recv, red_send, red_recv,
):
    rg = (rg_low, rg_high)
    terms, width = left_ops.shape[0], left_ops.shape[-1]
    nvec, sectors = w.shape[0], w.shape[1]
    part = width // planes // 2
    rows = nvec * part
    span = terms * part
    chunks = sectors // chunk
    all_terms = terms * planes
    plane = lax.axis_index("ops")
    place = lax.axis_index("sec")
    core = lax.rem(place, 2)
    chip = place // 2
    px, py = lax.rem(chip, side), chip // side
    first = px * (1 - core) + py * core
    second = py * (1 - core) + px * core

    def sector_of(one, two):
        x = one * (1 - core) + two * core
        y = two * (1 - core) + one * core
        return 2 * (y * side + x) + core

    def shift(base, offset, n):
        return lax.rem(base + (offset + n), n)

    above = [{"ops": shift(plane, d, planes)} for d in range(1, planes)]
    along = [{"sec": sector_of(shift(first, d, side), second)} for d in range(1, side)]
    across = [{"sec": sector_of(first, shift(second, d, side))} for d in range(1, side)]
    sibling = {"sec": place + 1 - 2 * core}

    barrier = pltpu.get_barrier_semaphore()
    partners = above + along + across + [sibling]
    for device in partners:
        pl.semaphore_signal(barrier, inc=1, device_id=device, device_id_type=MESH)

    loads = [
        pltpu.make_async_copy(a, b, in_sem.at[i])
        for i, (a, b) in enumerate([
            (right_hbm, right_ops), (kind_hbm, kind), (left_hbm, left_ops), (number_hbm, number), (w_hbm, w)
        ])
    ]
    for copy in loads:
        copy.start()

    lane = lax.broadcasted_iota(jnp.int32, (width, width), 1)
    sub_lane = lax.broadcasted_iota(jnp.int32, (width, width), 0)
    loads[0].wait()
    right_keep = (lane < right_dim[0]) & (sub_lane < right_dim[0])
    blocks = [jnp.where(right_keep, right_ops[k, 0].astype(F32), 0.0).T for k in range(terms)]
    for o in range(planes):
        for h in range(2):
            low = (h * planes + o) * part
            rt[h, o] = jnp.concatenate([block[low:low + part] for block in blocks], axis=0).astype(BF16)

    def at(c, one, two):
        return (c * side + one) * side + two

    mine = at(core, first, second)

    def slot(h, o):
        return rg[h].at[mine, pl.ds(pl.multiple_of(o * span, span), span)]

    for h in range(2):
        rg[h][mine, pl.ds(pl.multiple_of(plane * span, span), span)] = rt[h, plane]

    pl.semaphore_wait(barrier, len(partners))

    def wait_for(ref, semaphore):
        remote(ref, ref, semaphore, semaphore, sibling).wait_recv()

    far_first = sorted(range(1, planes), key=lambda d: -min(d, planes - d))
    def slices(h):
        for d in far_first:
            to = shift(plane, d, planes)
            remote(rt.at[h, to], slot(h, plane), a2a_send.at[h], a2a_recv.at[h], {"ops": to}).start()

    slices(0)
    for copy in loads[1:3]:
        copy.wait()
    left_keep = (lane < left_dim[0]) & (sub_lane < left_dim[0])
    for k in range(terms):
        block = jnp.where(left_keep, left_ops[k, 0].astype(F32), 0.0)
        normal = (jnp.zeros((width, width), jnp.int32) + kind[k]) == 0
        lg[plane, k * width:(k + 1) * width] = jnp.where(normal, block.T, block).astype(BF16)


    pieces = 2
    deep = terms * width // pieces

    def left_ring(i):
        return Ring(
            planes, plane, lambda q: {"ops": q},
            lambda q: lg.at[q, pl.ds(i * deep, deep)],
            lambda q, h: lg.at[q, pl.ds(i * deep + h * (deep // 2), deep // 2)],
            left_send.at[0], lambda index: left_recv.at[i, index],
        )

    left = [left_ring(i) for i in range(pieces)]

    def left_step(d):
        for each in left:
            each.step(d)


    order = [d for d in (1, 3, 2) if d < side]

    def first_sends(h):
        block = rg[h].at[mine]
        for d in reversed(order):
            remote(block, block, first_send.at[h], first_recv.at[h, d], along[d - 1]).start()

    def second_sends(h, j):
        block = rg[h].at[at(core, shift(first, -j, side), second)]
        for d in order:
            remote(block, block, second_send.at[h], second_recv.at[h, j], across[d - 1]).start()

    def line_arrival(h, j):
        wait_for(rg[h].at[pl.ds(0, side - 1)], second_recv.at[h, j])
        line = rg[h].at[pl.ds(at(core, shift(first, -j, side), 0), side)]
        remote(line, line, sib_send.at[h], sib_recv.at[h], sibling).start()

    for copy in loads[3:]:
        copy.wait()
    pick_row = lax.broadcasted_iota(jnp.int32, (2 * part, width), 0)
    pick_lane = lax.broadcasted_iota(jnp.int32, (2 * part, width), 1)
    pick = jnp.where(
        pick_lane == (pick_row // part * planes + plane) * part + lax.rem(pick_row, part), 1.0, 0.0
    ).astype(BF16)

    def pick_sectors(low, high):
        for s in range(low, high):
            picked[s] = lax.dot_general(
                pick, w[:, s].reshape(nvec * width, width), (((1,), (1,)), ((), ())), preferred_element_type=F32
            )

    def first_arrivals(h):
        for j in order:
            wait_for(rg[h].at[0], first_recv.at[h, j])
            second_sends(h, j)

    pick_sectors(0, 8)
    slices(1)
    for each in left:
        each.start()
    wait_for(rt.at[0, pl.ds(0, planes - 1)], a2a_recv.at[0])
    first_sends(0)
    pick_sectors(8, 16)
    second_sends(0, 0)
    wait_for(rt.at[1, pl.ds(0, planes - 1)], a2a_recv.at[1])
    first_sends(1)
    left_step(1)
    first_arrivals(0)
    second_sends(1, 0)
    left_step(2)
    first_arrivals(1)
    line_arrival(0, 0)
    left_step(3)
    pick_sectors(16, sectors)
    for j in order:
        line_arrival(0, j)
    left_step(4)
    half_blocks = side * side
    wait_for(rg[0].at[pl.ds(0, half_blocks)], sib_recv.at[0])

    def sigma_ring(h, j):
        half = chunk * rows // 2
        return Ring(
            planes, plane, lambda q: {"ops": q},
            lambda q: sg.at[h, j, q], lambda q, way: sg.at[h, j, q, pl.ds(way * half, half)],
            sigma_send.at[0], lambda index: sigma_recv.at[h, j, index],
        )

    sigma_rings = [[sigma_ring(h, j) for j in range(chunks)] for h in range(2)]
    traces = [[jnp.zeros((part, width), F32) for _ in range(nvec)] for _ in range(nvec)]

    def right_of(s):
        r = number[s]
        c = lax.rem(r, 2)
        x, y = lax.rem(r // 2, side), r // 2 // side
        return at(c, x * (1 - c) + y * c, y * (1 - c) + x * c)

    def compute(h, j):
        for i in range(chunk):
            s = j * chunk + i
            product = lax.dot_general(
                rg[h][right_of(s)], w[:, s].reshape(nvec * width, width), (((1,), (1,)), ((), ())),
                preferred_element_type=F32,
            ).reshape(all_terms, part, nvec * width)
            product = jnp.concatenate(
                [product[:, :, v * width:(v + 1) * width] for v in range(nvec)], axis=1
            ).astype(BF16)
            for k in range(all_terms):
                inner[i * rows:(i + 1) * rows, k * width:(k + 1) * width] = product[k]
        total = jnp.dot(
            inner[...], lg[...].reshape(all_terms * width, width), preferred_element_type=F32
        ).astype(BF16)
        sg[h, j, plane] = total
        sigma_rings[h][j].start()

    def trace(h, j):
        total = sg[h, j, plane].astype(F32).reshape(chunk, nvec, part, width)
        for i in range(nvec):
            other = picked[j * chunk:(j + 1) * chunk, h * part:(h + 1) * part, i * width:(i + 1) * width]
            for v in range(nvec):
                traces[i][v] = traces[i][v] + jnp.sum(other * total[:, v], axis=0)

    def sigma_step(h, d):
        for j in range(chunks):
            sigma_rings[h][j].step(d)

    def assemble(j):
        for i in range(chunk):
            halves = [
                sg[h, j, :, i * rows:(i + 1) * rows].astype(F32).reshape(planes, nvec, part, width) for h in range(2)
            ]
            for v in range(nvec):
                joined = jnp.concatenate([half[:, v].reshape(planes * part, width) for half in halves], axis=0)
                out[v, j * chunk + i] = joined.astype(BF16).T

    stages = [(plane, planes, above), (first, side, along), (second, side, across), (core, 2, [sibling])]

    def reduce_sends(stage):
        me, n, devices = stages[stage]
        for d in range(1, n):
            remote(
                red.at[stage, me], red.at[stage, me], red_send.at[stage], red_recv.at[stage], devices[d - 1]
            ).start()

    def subspace_start():
        tile_row = lax.broadcasted_iota(jnp.int32, red.shape[-2:], 0)
        tile_column = lax.broadcasted_iota(jnp.int32, red.shape[-2:], 1)
        tile = jnp.zeros(red.shape[-2:], F32)
        for i in range(nvec):
            for v in range(nvec):
                value = jnp.sum(traces[i][v], axis=(0, 1), keepdims=True)
                tile = tile + jnp.where((tile_row == i) & (tile_column == v), value, 0.0)
        red[0, plane] = tile
        reduce_sends(0)

    def subspace_stage(stage):
        _, n, _ = stages[stage]
        wait_for(red.at[stage, pl.ds(0, n - 1)], red_recv.at[stage])
        total = red[stage, 0]
        for i in range(1, n):
            total = total + red[stage, i]
        if stage + 1 < len(stages):
            red[stage + 1, stages[stage + 1][0]] = total
            reduce_sends(stage + 1)
        else:
            sub[...] = total * (1.0 / math.sqrt(2 * side * side * sectors * width * width))

    for j in range(chunks):
        compute(0, j)
    for j in range(chunks):
        trace(0, j)
    for j in [0] + order:
        line_arrival(1, j)
    sigma_step(0, 1)
    wait_for(rg[1].at[pl.ds(0, half_blocks)], sib_recv.at[1])
    for j in range(chunks):
        compute(1, j)
    for j in range(chunks):
        trace(1, j)
    subspace_start()
    sigma_step(0, 2)
    sigma_step(1, 1)
    sigma_step(0, 3)
    subspace_stage(0)
    sigma_step(1, 2)
    sigma_step(0, 4)
    subspace_stage(1)
    sigma_step(1, 3)
    subspace_stage(2)

    for h in range(2):
        wait_for(rt.at[h, pl.ds(0, planes - 1)], a2a_send.at[h])
        wait_for(rg[h].at[pl.ds(0, side - 1)], first_send.at[h])
        wait_for(rg[h].at[pl.ds(0, side * (side - 1))], second_send.at[h])
        wait_for(rg[h].at[pl.ds(0, half_blocks)], sib_send.at[h])
    wait_for(lg.at[pl.ds(0, planes - 1)], left_send.at[0])
    for j in range(chunks):
        sigma_rings[1][j].step(4)
        assemble(j)
        if j == 0:
            subspace_stage(3)
    wait_for(sg.at[:, :, pl.ds(0, planes - 1)], sigma_send.at[0])
    for stage, (_, n, _) in enumerate(stages):
        wait_for(red.at[stage, pl.ds(0, n - 1)], red_send.at[stage])


def body(wavefunction, right_number, left_dim, right_dim, left_ops, right_ops, set_kind, *, chunk=16):
    nvec, sectors, width, _ = wavefunction.shape
    planes = lax.axis_size("ops")
    places = lax.axis_size("sec")
    side = math.isqrt(places // 2)
    terms = left_ops.shape[0]
    part = width // planes // 2
    rows = nvec * part
    chunks = sectors // chunk
    vmem = pl.BlockSpec(memory_space=pltpu.VMEM)
    smem = pl.BlockSpec(memory_space=pltpu.SMEM)
    hbm = pl.BlockSpec(memory_space=pltpu.HBM)
    dma = pltpu.SemaphoreType.DMA
    out, sub = pl.pallas_call(
        functools.partial(kernel, planes, side, chunk),
        out_shape=(
            jax.ShapeDtypeStruct(wavefunction.shape, BF16),
            jax.ShapeDtypeStruct((8, 128), F32),
        ),
        in_specs=[smem] * 2 + [hbm] * 5,
        out_specs=(vmem, vmem),
        scratch_shapes=[
            pltpu.VMEM(wavefunction.shape, BF16),
            pltpu.SMEM((sectors,), jnp.int32),
            pltpu.SMEM(set_kind.shape, jnp.int32),
            pltpu.VMEM(left_ops.shape, BF16),
            pltpu.VMEM(right_ops.shape, BF16),
            pltpu.VMEM((2, planes, terms * part, width), BF16),
            pltpu.VMEM((places, planes * terms * part, width), BF16),
            pltpu.VMEM((places, planes * terms * part, width), BF16),
            pltpu.VMEM((planes, terms * width, width), BF16),
            pltpu.VMEM((chunk * rows, planes * terms * width), BF16),
            pltpu.VMEM((2, chunks, planes, chunk * rows, width), BF16),
            pltpu.VMEM((sectors, 2 * part, nvec * width), F32),
            pltpu.VMEM((4, max(planes, side, 2), 8, 128), F32),
            dma((5,)),
            dma((2,)),
            dma((2,)),
            dma((2,)),
            dma((2, side)),
            dma((2,)),
            dma((2, side)),
            dma((1,)),
            dma((2, planes)),
            dma((1,)),
            dma((2, chunks, planes)),
            dma((2,)),
            dma((2,)),
            dma((4,)),
            dma((4,)),
        ],
        compiler_params=pltpu.CompilerParams(
            collective_id=0, has_side_effects=True, vmem_limit_bytes=48 * 1024 * 1024
        ),
        cost_estimate=pl.CostEstimate(
            flops=4 * sectors * nvec * terms * width**3, bytes_accessed=6 * 1024 * 1024, transcendentals=0
        ),
    )(left_dim, right_dim, *[
        pltpu.with_memory_space_constraint(each, pltpu.HBM)
        for each in (
            wavefunction, right_number.reshape(sectors), set_kind, left_ops, right_ops
        )
    ])
    return out, sub[:nvec, :nvec]


def solution(mesh):
    return jax.shard_map(
        body,
        mesh=mesh,
        in_specs=(
            P(None, "sec", None, None),
            P("sec", None),
            P("sec"),
            P("sec"),
            P("ops", "sec", None, None),
            P("ops", "sec", None, None),
            P("ops"),
        ),
        out_specs=(P(None, "sec", None, None), P()),
        check_vma=False,
    )
```
